512 devices in a mesh: dp: 32 (over x, y), seq: 16 (over z, core).
Axes of the slice: x: 4, y: 8, z: 8, core: 2. Of those that a mesh axis runs over, the one named last changes fastest.
Arguments:
- projected: bfloat16 [163840, 6144], P(('dp', 'seq')), parts along dimension 0, may hold values from -16 to 16, as said below
- kept_index: int32 [81920], P('dp'), parts along dimension 0, may hold values from 0 to 5119, as said below
Outputs:
- attended: bfloat16 [81920, 2048], P(('dp', 'seq')), parts along dimension 0
The draws below stay inside these ranges and needn't reach their ends.
There are 32 independent parts, one for each index of `dp`. The reference program is written for one: setup_inputs(seed, part) draws one part's arguments, and reference() takes and returns one part's arrays. A program takes and returns all parts, laid end to end along the dimension named above; each array names one. Nothing has to cross between parts.
Inputs may be any that keep to these rules, and one draw needn't show every extreme that they name: `kept_index`: strictly ascending. With P(t) the number of entries below t * 320, P(t) - t * 160 lies within -80 to 80 for every tile t, and both ends are reached in every draw; a tile may keep from none to all of its tokens. `projected`: real values.
All inputs are finite; a program needn't handle non-finite values.
Results may differ from the reference program's by a relative error of at most 0.0048.
Values may be sent and summed in bfloat16 or wider, within the bound.
No kernel may reach another device: no remote copies, remote signals or barrier semaphores. Data moves between devices by JAX's collectives and lax.ppermute only.
A program may use at most 64 MiB of HBM per device.

```python
import jax
import jax.numpy as jnp
from jax import lax

H = 16
HD = 128
TILE = 320
TOKENS = 5120
KEPT = 2560


def shuffle_tile(subkey):
    return jax.random.permutation(subkey, TILE)


def draw_kept_index(key, part):
    key = jax.random.fold_in(key, 11)
    key_inner, key_high, key_step, key_shuffle = jax.random.split(key, 4)
    tile_count = TOKENS // TILE
    shard_rows = TILE // 2
    spread = TILE // 4
    inner = jax.random.randint(key_inner, (tile_count - 1,), -spread, spread + 1)
    highest = jax.random.randint(key_high, (), 0, tile_count - 1)
    stride = jax.random.randint(key_step, (), 1, tile_count - 1)
    lowest = (highest + stride) % (tile_count - 1)
    spots = jnp.arange(tile_count - 1)
    inner = jnp.where(spots == highest, spread, jnp.where(spots == lowest, -spread, inner))
    edge = jnp.zeros((1,), jnp.int32)
    drift = jnp.concatenate([edge, inner.astype(jnp.int32), edge])
    counts = shard_rows + drift[1:] - drift[:-1]
    shuffled = jax.vmap(shuffle_tile)(jax.random.split(key_shuffle, tile_count))
    placing = jnp.argsort(shuffled, axis=1)
    chosen = (placing < counts[:, None]).reshape(-1)
    ranking = jnp.where(chosen, 0, TOKENS) + jnp.arange(TOKENS)
    return jnp.argsort(ranking)[:TOKENS // 2].astype(jnp.int32)


def draw_projected(key, part):
    key = jax.random.fold_in(key, 23)
    key_base = jax.random.fold_in(key, 0)
    width = H * HD
    values = jnp.clip(jax.random.normal(key_base, (TOKENS, 3 * width), jnp.float32), -6.0, 6.0)
    return values.astype(jnp.bfloat16)


def setup_inputs(seed: int = 0, part: int = 0) -> dict:
    key_list = jax.random.split(jax.random.key(seed), 3)
    own_keys = jax.random.split(jax.random.fold_in(key_list[2], part), 3)
    return {
        "projected": draw_projected(jax.random.fold_in(jax.random.fold_in(key_list[2], part), 71), part),
        "kept_index": draw_kept_index(jax.random.fold_in(jax.random.fold_in(key_list[2], part), 71), part),
    }


def single_head(triple):
    queries = triple[0]
    key_rows = triple[1]
    value_rows = triple[2]
    scores = jnp.dot(queries, key_rows.T, preferred_element_type=jnp.float32) * (HD ** -0.5)
    row_max = jnp.max(scores, axis=-1, keepdims=True)
    weights = jnp.exp(scores - row_max)
    totals = jnp.sum(weights, axis=-1, keepdims=True)
    mixed = jnp.dot(weights.astype(jnp.bfloat16), value_rows, preferred_element_type=jnp.float32)
    return (mixed / totals).astype(jnp.bfloat16)


def reference(projected, kept_index):
    gathered = jnp.take(projected, kept_index, axis=0)
    stacked = gathered.reshape(KEPT, 3, H, HD)
    per_head = jnp.transpose(stacked, (2, 1, 0, 3))
    outputs = lax.map(single_head, per_head)
    return jnp.transpose(outputs, (1, 0, 2)).reshape(KEPT, H * HD)
```

```python
import functools

import jax
import jax.numpy as jnp
from jax import lax
from jax.experimental import pallas as pl
from jax.experimental.pallas import tpu as pltpu
from jax.sharding import PartitionSpec as P

H = 16
HD = 128
LOG2E = 1.4426950408889634
VMEM_BYTES = 50 * 1024 * 1024


def select_kernel(index_ref, q_ref, k_ref, v_ref, own_ref, left_ref, right_ref, choice):
    tokens = q_ref.shape[0]
    spill = left_ref.shape[1]
    rows = own_ref.shape[1]
    heads = own_ref.shape[0]

    @pl.when(pl.program_id(0) == 0)
    def _():
        token = lax.broadcasted_iota(jnp.int32, (tokens, choice.shape[0]), 0)
        hits = jnp.where(token == index_ref[...], 1.0, 0.0)
        choice[...] = jnp.transpose(hits).astype(jnp.bfloat16)

    for c, ref in enumerate((q_ref, k_ref, v_ref)):
        picked = jnp.dot(choice[...], ref[...], preferred_element_type=jnp.float32)
        picked = picked.astype(jnp.bfloat16)
        for h in range(heads):
            block = picked[:, h * HD : (h + 1) * HD]
            place = slice(c * HD, (c + 1) * HD)
            left_ref[h, :, place] = block[:spill]
            own_ref[h, :, place] = block[spill : spill + rows]
            right_ref[h, :, place] = block[spill + rows :]


def select_rows(projected, index_row, shard_rows, spill_rows):
    tokens, width = projected.shape
    groups = 4
    heads = H // groups
    slots = shard_rows + 2 * spill_rows

    def columns(c):
        return pl.BlockSpec((tokens, heads * HD), lambda g: (0, c * groups + g))

    def by_head(rows):
        return pl.BlockSpec((heads, rows, 3 * HD), lambda g: (g, 0, 0))

    def result(rows):
        return jax.ShapeDtypeStruct((H, rows, 3 * HD), projected.dtype)

    return pl.pallas_call(
        select_kernel,
        out_shape=(result(shard_rows), result(spill_rows), result(spill_rows)),
        grid=(groups,),
        in_specs=[pl.BlockSpec((1, slots), lambda g: (0, 0)), columns(0), columns(1), columns(2)],
        out_specs=(by_head(shard_rows), by_head(spill_rows), by_head(spill_rows)),
        scratch_shapes=[pltpu.VMEM((slots, tokens), jnp.bfloat16)],
        compiler_params=pltpu.CompilerParams(vmem_limit_bytes=VMEM_BYTES),
    )(index_row, projected, projected, projected)


def attend_kernel(q_ref, k_ref, v_ref, out_ref, *, block):
    key_rows = k_ref[...]
    ones = jnp.ones(v_ref.shape, v_ref.dtype)
    value_rows = jnp.concatenate([v_ref[...], ones], axis=1)
    scale = HD ** (-0.5) * LOG2E
    for start in range(0, q_ref.shape[0], block):
        queries = q_ref[start : start + block, :]
        scores = lax.dot_general(
            queries, key_rows, (((1,), (1,)), ((), ())), preferred_element_type=jnp.float32
        )
        row_max = jnp.max(scores, axis=-1, keepdims=True)
        weights = jnp.exp2((scores - row_max) * scale).astype(jnp.bfloat16)
        mixed = jnp.dot(weights, value_rows, preferred_element_type=jnp.float32)
        out_ref[start : start + block, :] = (mixed[:, :HD] / mixed[:, HD:]).astype(out_ref.dtype)


def attend(triples):
    total = triples.shape[0]

    def columns(c):
        return pl.BlockSpec((total, HD), lambda i: (0, c))

    return pl.pallas_call(
        functools.partial(attend_kernel, block=256),
        out_shape=jax.ShapeDtypeStruct((total, HD), triples.dtype),
        grid=(1,),
        in_specs=[columns(0), columns(1), columns(2)],
        out_specs=pl.BlockSpec((total, HD), lambda i: (0, 0)),
        compiler_params=pltpu.CompilerParams(vmem_limit_bytes=VMEM_BYTES),
    )(triples, triples, triples)


def passed_along(block, axis, distance):
    devices = range(lax.axis_size(axis))
    route = [(i - distance, i) for i in devices if i - distance in devices]
    return lax.ppermute(block, axis, route)


def local(projected, kept_index):
    device_count = lax.axis_size("seq")
    device_place = lax.axis_index("seq")
    tile_rows = projected.shape[0]
    kept_total = kept_index.shape[0]
    shard_rows = kept_total // device_count
    spill_rows = tile_rows // 4
    slots = shard_rows + 2 * spill_rows
    padded = jnp.pad(kept_index - device_place * tile_rows, (spill_rows, spill_rows), constant_values=-1)
    index_row = lax.dynamic_slice(padded, (device_place * shard_rows,), (slots,))[None, :]
    own, left_rows, right_rows = select_rows(projected, index_row, shard_rows, spill_rows)
    from_left = passed_along(right_rows, "seq", 1)
    from_right = passed_along(left_rows, "seq", -1)
    shard_data = own + jnp.concatenate([from_left, from_right], axis=1)
    triples = lax.all_to_all(shard_data, "seq", split_axis=0, concat_axis=0, tiled=True)
    attended = attend(triples.reshape(kept_total, 3 * HD))
    by_shard = attended.reshape(device_count, shard_rows, HD)
    returned = lax.all_to_all(by_shard, "seq", split_axis=0, concat_axis=0, tiled=True)
    return jnp.transpose(returned, (1, 0, 2)).reshape(shard_rows, H * HD)


def solution(mesh):
    return jax.shard_map(
        local,
        mesh=mesh,
        in_specs=(P(("dp", "seq"), None), P("dp")),
        out_specs=P(("dp", "seq"), None),
        check_vma=False,
    )
```

```python
import functools

import jax
import jax.numpy as jnp
from jax import lax
from jax.experimental import pallas as pl
from jax.experimental.pallas import tpu as pltpu
from jax.sharding import PartitionSpec as P

H = 16
HD = 128
CORES = 2
GROUPS = 4
LOG2E = 1.4426950408889634
VMEM_BYTES = 50 * 1024 * 1024


def choose(device, index_ref, tokens, rows, choice):
    kept = index_ref.shape[0]
    spill = rows // 2
    shift = lax.rem(spill - device * rows + kept, kept)
    index = pltpu.roll(jnp.broadcast_to(index_ref[...].reshape(1, kept), (8, kept)), shift, 1)
    index = index[:1, : 2 * rows] - device * tokens
    token = lax.broadcasted_iota(jnp.int32, (tokens, 2 * rows), 0)
    hits = jnp.transpose(jnp.where(token == index, 1.0, 0.0))
    groups = [hits[i : i + spill] for i in range(0, 2 * rows, spill)]
    odd = lax.rem(device, CORES) == 1
    for i in range(len(groups)):
        chosen = jnp.where(odd, groups[-1 - i], groups[i])
        choice[i * spill : (i + 1) * spill, :] = chosen.astype(jnp.bfloat16)


def select_kernel(place_ref, index_ref, q_ref, k_ref, v_ref, *refs, first):
    *out_refs, choice = refs
    tokens = q_ref.shape[0]

    @pl.when(pl.program_id(0) == 0)
    def _():
        choose(place_ref[0], index_ref, tokens, tokens // 2, choice)

    count = sum(ref.shape[1] for ref in out_refs)
    for c, ref in enumerate((q_ref, k_ref, v_ref)):
        picked = jnp.dot(choice[first : first + count, :], ref[...], preferred_element_type=jnp.float32)
        picked = picked.astype(jnp.bfloat16)
        start = 0
        for out_ref in out_refs:
            heads, rows, _ = out_ref.shape
            for h in range(heads):
                block = picked[start : start + rows, h * HD : (h + 1) * HD]
                out_ref[h, :, c * HD : (c + 1) * HD] = block
            start += rows


def select_rows(place, kept_index, projected, first, counts):
    tokens = projected.shape[0]
    heads = H // GROUPS

    def columns(c):
        return pl.BlockSpec((tokens, heads * HD), lambda g, place: (0, c * GROUPS + g))

    def by_head(rows):
        return pl.BlockSpec((heads, rows, 3 * HD), lambda g, place: (g, 0, 0))

    return pl.pallas_call(
        functools.partial(select_kernel, first=first),
        out_shape=[jax.ShapeDtypeStruct((H, rows, 3 * HD), projected.dtype) for rows in counts],
        grid_spec=pltpu.PrefetchScalarGridSpec(
            num_scalar_prefetch=1,
            grid=(GROUPS,),
            in_specs=[pl.BlockSpec(kept_index.shape, lambda g, place: (0,))] + [columns(c) for c in range(3)],
            out_specs=[by_head(rows) for rows in counts],
            scratch_shapes=[pltpu.VMEM((tokens, tokens), jnp.bfloat16)],
        ),
        compiler_params=pltpu.CompilerParams(vmem_limit_bytes=VMEM_BYTES),
    )(place, kept_index, projected, projected, projected)


def attend_kernel(q_ref, k_ref, v_ref, out_ref, *, block):
    key_rows = k_ref[...]
    ones = jnp.ones(v_ref.shape, v_ref.dtype)
    value_rows = jnp.concatenate([v_ref[...], ones], axis=1)
    scale = HD ** (-0.5) * LOG2E
    starts = range(0, q_ref.shape[0], block)

    half = block // 4

    def scores_of(start):
        middle, last = start + 2 * half, start + 3 * half
        queries = jnp.concatenate(
            [q_ref[start:middle, :], q_ref[last : last + half, :], q_ref[middle:last, :]], axis=0
        )
        return lax.dot_general(
            queries, key_rows, (((1,), (1,)), ((), ())), preferred_element_type=jnp.float32
        )

    def weights_of(scores):
        row_max = jnp.max(scores, axis=-1, keepdims=True)
        return jnp.exp2((scores - row_max) * scale).astype(jnp.bfloat16)

    def write(start, weights):
        mixed = jnp.dot(weights, value_rows, preferred_element_type=jnp.float32)
        out_ref[start : start + block, :] = (mixed[:, :HD] / mixed[:, HD:]).astype(out_ref.dtype)

    scores = scores_of(0)
    weights = None
    for start in starts:
        later = scores_of(start + block) if start + block < starts.stop else None
        newer = weights_of(scores)
        if weights is not None:
            write(start - block, weights)
        scores, weights = later, newer
    write(starts[-1], weights)


def attend(triples, shard_rows):
    total = triples.shape[0]

    def columns(c):
        return pl.BlockSpec((total, HD), lambda i: (0, c))

    return pl.pallas_call(
        functools.partial(attend_kernel, block=CORES * shard_rows),
        out_shape=jax.ShapeDtypeStruct((total, HD), triples.dtype),
        grid=(1,),
        in_specs=[columns(0), columns(1), columns(2)],
        out_specs=pl.BlockSpec((total, HD), lambda i: (0, 0)),
        compiler_params=pltpu.CompilerParams(vmem_limit_bytes=VMEM_BYTES),
    )(triples, triples, triples)


def local(projected, kept_index):
    device_count = lax.axis_size("seq")
    place = lax.axis_index("seq").astype(jnp.int32)[None]
    kept_total = kept_index.shape[0]
    shard_rows = kept_total // device_count
    spill_rows = projected.shape[0] // 4
    across = [(i, i - 1 + 2 * (i % 2)) for i in range(1, device_count - 1)]
    within = [(i, i ^ 1) for i in range(device_count)]
    (inter,) = select_rows(place, kept_index, projected, 0, [spill_rows])
    from_across = lax.ppermute(inter, "seq", across)
    own, intra = select_rows(place, kept_index, projected, spill_rows, [shard_rows, spill_rows])
    from_within = lax.ppermute(intra, "seq", within)
    shard_data = own + jnp.concatenate([from_across, from_within], axis=1)
    triples = lax.all_to_all(shard_data, "seq", split_axis=0, concat_axis=0, tiled=True)
    attended = attend(triples.reshape(kept_total, 3 * HD), shard_rows)
    by_shard = attended.reshape(device_count, shard_rows, HD)
    returned = lax.all_to_all(by_shard, "seq", split_axis=0, concat_axis=0, tiled=True)
    return jnp.transpose(returned, (1, 0, 2)).reshape(shard_rows, H * HD)


def solution(mesh):
    return jax.shard_map(
        local,
        mesh=mesh,
        in_specs=(P(("dp", "seq"), None), P("dp")),
        out_specs=P(("dp", "seq"), None),
        check_vma=False,
    )
```

```python
import functools

import jax
import jax.numpy as jnp
from jax import lax
from jax.experimental import pallas as pl
from jax.experimental.pallas import tpu as pltpu
from jax.sharding import PartitionSpec as P

H = 16
HD = 128
CORES = 2
NEAR = 4
LOG2E = 1.4426950408889634
VMEM_BYTES = 50 * 1024 * 1024


def pick(device, index_ref, start, tokens, count):
    kept = index_ref.shape[0]
    shift = lax.rem(2 * kept - start, kept)
    index = pltpu.roll(jnp.broadcast_to(index_ref[...].reshape(1, kept), (8, kept)), shift, 1)
    index = (index[:, :128] - device * tokens).astype(jnp.float32)
    column = jnp.transpose(index)[:count, :1]
    token = lax.broadcasted_iota(jnp.int32, (count, tokens), 1).astype(jnp.float32)
    return jnp.where(token == column, 1.0, 0.0).astype(jnp.bfloat16)


def spill_kernel(index_ref, tile_ref, out_ref, columns, sems):
    heads, spill, _ = out_ref.shape
    tokens = tile_ref.shape[0]
    kinds, _, width = columns.shape
    copies = []
    for c in range(kinds):
        at = pl.ds(c * width, width)
        copies.append(pltpu.make_async_copy(tile_ref.at[:, at], columns.at[c], sems.at[c]))
        copies[-1].start()
    device = lax.axis_index("seq")
    odd = lax.rem(device, CORES)
    start = (2 * device + odd * 2 + (1 - odd) * -1) * spill
    choice = pick(device, index_ref, start, tokens, spill)
    for c in range(kinds):
        copies[c].wait()
        picked = jnp.dot(choice, columns[c], preferred_element_type=jnp.float32)
        picked = picked.astype(jnp.bfloat16)
        for h in range(heads):
            out_ref[h, :, c * HD : (c + 1) * HD] = picked[:, h * HD : (h + 1) * HD]


def select_spill(kept_index, projected, spill_rows):
    tokens = projected.shape[0]
    vmem = pl.BlockSpec(memory_space=pltpu.VMEM)
    return pl.pallas_call(
        spill_kernel,
        out_shape=jax.ShapeDtypeStruct((H, spill_rows, 3 * HD), projected.dtype),
        in_specs=[vmem, pl.BlockSpec(memory_space=pltpu.HBM)],
        out_specs=vmem,
        scratch_shapes=[
            pltpu.VMEM((3, tokens, H * HD), projected.dtype),
            pltpu.SemaphoreType.DMA((3,)),
        ],
        compiler_params=pltpu.CompilerParams(vmem_limit_bytes=VMEM_BYTES),
    )(kept_index, projected)


def select_kernel(index_ref, q_ref, k_ref, v_ref, *refs, groups, parts):
    *out_refs, choice = refs
    tokens = q_ref.shape[0]
    spill = tokens // 4

    @pl.when(pl.program_id(0) == 0)
    def _():
        device = lax.axis_index("seq")
        odd = lax.rem(device, CORES)
        for i, group in enumerate(groups):
            ahead = odd * (2 - group) + (1 - odd) * (group - 1)
            start = (2 * device + ahead) * spill
            choice[i * spill : (i + 1) * spill, :] = pick(device, index_ref, start, tokens, spill)

    for c, ref in enumerate((q_ref, k_ref, v_ref)):
        picked = jnp.dot(choice[...], ref[...], preferred_element_type=jnp.float32)
        picked = picked.astype(jnp.bfloat16)
        for out_ref, (start, rows, columns) in zip(out_refs, parts):
            if c not in columns:
                continue
            at = columns.index(c) * HD
            for h in range(out_ref.shape[0]):
                out_ref[h, :, at : at + HD] = picked[start : start + rows, h * HD : (h + 1) * HD]


def select_rows(kept_index, projected, groups, parts, steps):
    tokens = projected.shape[0]
    heads = H // steps

    def columns(c):
        return pl.BlockSpec((tokens, heads * HD), lambda g: (0, c * steps + g))

    def by_head(rows, width):
        return pl.BlockSpec((heads, rows, width), lambda g: (g, 0, 0))

    return pl.pallas_call(
        functools.partial(select_kernel, groups=groups, parts=parts),
        out_shape=[
            jax.ShapeDtypeStruct((H, rows, len(cols) * HD), projected.dtype) for _, rows, cols in parts
        ],
        grid=(steps,),
        in_specs=[pl.BlockSpec(kept_index.shape, lambda g: (0,))] + [columns(c) for c in range(3)],
        out_specs=[by_head(rows, len(cols) * HD) for _, rows, cols in parts],
        scratch_shapes=[pltpu.VMEM((len(groups) * tokens // 4, tokens), jnp.bfloat16)],
        compiler_params=pltpu.CompilerParams(vmem_limit_bytes=VMEM_BYTES),
    )(kept_index, projected, projected, projected)


def attend_kernel(triple_ref, *refs, near, shard_rows):
    if near:
        *out_refs, queries_ref, result_ref = refs
    else:
        out_ref, queries_ref, result_ref, zeros_ref, sems = refs
    total = triple_ref.shape[0]
    key_rows = triple_ref[:, HD : 2 * HD]
    ones = jnp.ones((total, HD), triple_ref.dtype)
    value_rows = jnp.concatenate([triple_ref[:, 2 * HD :], ones], axis=1)
    scale = HD ** (-0.5) * LOG2E
    half = shard_rows // 2
    block = 2 * shard_rows
    device = lax.axis_index("seq")
    count = queries_ref.shape[0] // shard_rows

    def shard_of(i):
        return device ^ (i if near else NEAR + i)

    for i in range(count):
        shard = shard_of(i)
        odd = lax.rem(shard, 2)
        for j, at in enumerate((odd, 1 - odd)):
            rows = pl.multiple_of(shard * shard_rows + at * half, 16)
            start = i * shard_rows + j * half
            queries_ref[start : start + half, :] = triple_ref[pl.ds(rows, half), :HD]

    def scores_of(start):
        return lax.dot_general(
            queries_ref[start : start + block, :],
            key_rows,
            (((1,), (1,)), ((), ())),
            preferred_element_type=jnp.float32,
        )

    def weights_of(scores):
        row_max = jnp.max(scores, axis=-1, keepdims=True)
        return jnp.exp2((scores - row_max) * scale).astype(jnp.bfloat16)

    copies = []

    def send(source, shard):
        copies.append(pltpu.make_async_copy(source, out_ref.at[shard], sems.at[len(copies)]))
        copies[-1].start()

    if not near:
        zeros_ref[...] = jnp.zeros_like(zeros_ref)
        for i in range(NEAR):
            send(zeros_ref, device ^ i)

    def write(start, weights):
        mixed = jnp.dot(weights, value_rows, preferred_element_type=jnp.float32)
        result = mixed[:, :HD] / mixed[:, HD:]
        result_ref[start : start + block, :] = result.astype(result_ref.dtype)
        for at in range(start, start + block, shard_rows):
            if near:
                out_refs[at // shard_rows][...] = result_ref[at : at + shard_rows, :]
            else:
                send(result_ref.at[at : at + shard_rows, :], shard_of(at // shard_rows))

    starts = range(0, count * shard_rows, block)
    scores = scores_of(0)
    weights = None
    for start in starts:
        later = scores_of(start + block) if start + block < starts.stop else None
        newer = weights_of(scores)
        if weights is not None:
            write(start - block, weights)
        scores, weights = later, newer
    write(starts[-1], weights)

    for copy in copies:
        copy.wait()


def attend(triples, shard_rows, near):
    total = triples.shape[0]
    shards = total // shard_rows
    whole = pl.BlockSpec(memory_space=pltpu.VMEM)
    if near:
        shape, outs, count, more = (shard_rows, HD), NEAR, NEAR, []
    else:
        more = [pltpu.VMEM((shard_rows, HD), triples.dtype), pltpu.SemaphoreType.DMA((shards,))]
        shape, outs, count = (shards, shard_rows, HD), 1, shards - NEAR
    return pl.pallas_call(
        functools.partial(attend_kernel, near=near, shard_rows=shard_rows),
        out_shape=[jax.ShapeDtypeStruct(shape, triples.dtype)] * outs,
        in_specs=[whole],
        out_specs=[whole if near else pl.BlockSpec(memory_space=pltpu.HBM)] * outs,
        scratch_shapes=[pltpu.VMEM((count * shard_rows, HD), triples.dtype)] * 2 + more,
        compiler_params=pltpu.CompilerParams(vmem_limit_bytes=VMEM_BYTES),
    )(triples)


def assemble_kernel(far_ref, *refs):
    *near_refs, out_ref, sems = refs
    heads = far_ref.shape[0]
    device = lax.axis_index("seq")
    copies = []

    def put(source, head):
        column = pl.multiple_of(head * HD, HD)
        at = len(copies)
        copies.append(pltpu.make_async_copy(source, out_ref.at[:, pl.ds(column, HD)], sems.at[at]))
        copies[-1].start()

    for i in range(NEAR, heads):
        put(far_ref.at[device ^ i], device ^ i)
    for m, ref in enumerate(near_refs):
        put(ref, device ^ m)
    for copy in copies:
        copy.wait()


def assemble(far, near):
    heads, rows, _ = far.shape
    whole = pl.BlockSpec(memory_space=pltpu.VMEM)
    return pl.pallas_call(
        assemble_kernel,
        out_shape=jax.ShapeDtypeStruct((rows, heads * HD), far.dtype),
        in_specs=[whole] * (1 + NEAR),
        out_specs=pl.BlockSpec(memory_space=pltpu.HBM),
        scratch_shapes=[pltpu.SemaphoreType.DMA((heads,))],
        compiler_params=pltpu.CompilerParams(vmem_limit_bytes=VMEM_BYTES),
    )(far, *near)


def local(projected, kept_index):
    device_count = lax.axis_size("seq")
    kept_total = kept_index.shape[0]
    shard_rows = kept_total // device_count
    spill_rows = projected.shape[0] // 4
    across = [(i, i - 1 + 2 * (i % 2)) for i in range(1, device_count - 1)]
    within = [(i, i ^ 1) for i in range(device_count)]
    everything = (0, 1, 2)
    own_parts = [(0, shard_rows, everything), (shard_rows, spill_rows, everything)]
    inter = select_spill(kept_index, projected, spill_rows)
    from_across = lax.ppermute(inter, "seq", across)
    own, intra = select_rows(kept_index, projected, (1, 2, 3), own_parts, 4)
    from_within = lax.ppermute(intra, "seq", within)
    shard_data = own + jnp.concatenate([from_across, from_within], axis=1)
    triples = lax.all_to_all(shard_data, "seq", split_axis=0, concat_axis=0, tiled=True)
    triples = triples.reshape(kept_total, 3 * HD)
    (far,) = attend(triples, shard_rows, False)
    far = lax.all_to_all(far, "seq", split_axis=0, concat_axis=0, tiled=True)
    near = list(attend(triples, shard_rows, True))
    for m in range(1, NEAR):
        near[m] = lax.ppermute(near[m], "seq", [(i, i ^ m) for i in range(device_count)])
    return assemble(far, near)


def solution(mesh):
    return jax.shard_map(
        local,
        mesh=mesh,
        in_specs=(P(("dp", "seq"), None), P("dp")),
        out_specs=P(("dp", "seq"), None),
        check_vma=False,
    )
```

```python
import functools

import jax
import jax.numpy as jnp
from jax import lax
from jax.experimental import pallas as pl
from jax.experimental.pallas import tpu as pltpu
from jax.sharding import PartitionSpec as P

H = 16
HD = 128
CORES = 2
NEAR = 5
NEAR_BLOCKS = (3, 2)
FAR_BLOCKS = (3, 3, 3, 2)
LOG2E = 1.4426950408889634
VMEM_BYTES = 50 * 1024 * 1024


def pick(device, index_ref, start, tokens, count):
    kept = index_ref.shape[0]
    shift = lax.rem(2 * kept - start, kept)
    index = pltpu.roll(jnp.broadcast_to(index_ref[...].reshape(1, kept), (8, kept)), shift, 1)
    index = (index[:, :128] - device * tokens).astype(jnp.float32)
    column = jnp.transpose(index)[:count, :1]
    token = lax.broadcasted_iota(jnp.int32, (count, tokens), 1).astype(jnp.float32)
    return jnp.where(token == column, 1.0, 0.0).astype(jnp.bfloat16)


def spill_kernel(index_ref, tile_ref, out_ref, columns, sems):
    heads, spill, _ = out_ref.shape
    tokens = tile_ref.shape[0]
    kinds, _, width = columns.shape
    copies = []
    for c in range(kinds):
        at = pl.ds(c * width, width)
        copies.append(pltpu.make_async_copy(tile_ref.at[:, at], columns.at[c], sems.at[c]))
        copies[-1].start()
    device = lax.axis_index("seq")
    odd = lax.rem(device, CORES)
    start = (2 * device + odd * 2 + (1 - odd) * -1) * spill
    choice = pick(device, index_ref, start, tokens, spill)
    for c in range(kinds):
        copies[c].wait()
        picked = jnp.dot(choice, columns[c], preferred_element_type=jnp.float32)
        picked = picked.astype(jnp.bfloat16)
        for h in range(heads):
            out_ref[h, :, c * HD : (c + 1) * HD] = picked[:, h * HD : (h + 1) * HD]


def select_spill(kept_index, projected, spill_rows):
    tokens = projected.shape[0]
    vmem = pl.BlockSpec(memory_space=pltpu.VMEM)
    return pl.pallas_call(
        spill_kernel,
        out_shape=jax.ShapeDtypeStruct((H, spill_rows, 3 * HD), projected.dtype),
        in_specs=[vmem, pl.BlockSpec(memory_space=pltpu.HBM)],
        out_specs=vmem,
        scratch_shapes=[
            pltpu.VMEM((3, tokens, H * HD), projected.dtype),
            pltpu.SemaphoreType.DMA((3,)),
        ],
        compiler_params=pltpu.CompilerParams(vmem_limit_bytes=VMEM_BYTES),
    )(kept_index, projected)


def select_kernel(index_ref, q_ref, k_ref, v_ref, *refs, groups, parts):
    *out_refs, choice = refs
    tokens = q_ref.shape[0]
    spill = tokens // 4

    @pl.when(pl.program_id(0) == 0)
    def _():
        device = lax.axis_index("seq")
        odd = lax.rem(device, CORES)
        for i, group in enumerate(groups):
            ahead = odd * (2 - group) + (1 - odd) * (group - 1)
            start = (2 * device + ahead) * spill
            choice[i * spill : (i + 1) * spill, :] = pick(device, index_ref, start, tokens, spill)

    for c, ref in enumerate((q_ref, k_ref, v_ref)):
        picked = jnp.dot(choice[...], ref[...], preferred_element_type=jnp.float32)
        picked = picked.astype(jnp.bfloat16)
        for out_ref, (start, rows, columns) in zip(out_refs, parts):
            if c not in columns:
                continue
            at = columns.index(c) * HD
            for h in range(out_ref.shape[0]):
                out_ref[h, :, at : at + HD] = picked[start : start + rows, h * HD : (h + 1) * HD]


def select_rows(kept_index, projected, groups, parts, steps):
    tokens = projected.shape[0]
    heads = H // steps

    def columns(c):
        return pl.BlockSpec((tokens, heads * HD), lambda g: (0, c * steps + g))

    def by_head(rows, width):
        return pl.BlockSpec((heads, rows, width), lambda g: (g, 0, 0))

    return pl.pallas_call(
        functools.partial(select_kernel, groups=groups, parts=parts),
        out_shape=[
            jax.ShapeDtypeStruct((H, rows, len(cols) * HD), projected.dtype) for _, rows, cols in parts
        ],
        grid=(steps,),
        in_specs=[pl.BlockSpec(kept_index.shape, lambda g: (0,))] + [columns(c) for c in range(3)],
        out_specs=[by_head(rows, len(cols) * HD) for _, rows, cols in parts],
        scratch_shapes=[pltpu.VMEM((len(groups) * tokens // 4, tokens), jnp.bfloat16)],
        compiler_params=pltpu.CompilerParams(vmem_limit_bytes=VMEM_BYTES),
    )(kept_index, projected, projected, projected)


def attend_kernel(triple_ref, *refs, near, shard_rows):
    if near:
        *out_refs, queries_ref, result_ref = refs
    else:
        out_ref, queries_ref, result_ref, zeros_ref, sems = refs
    total = triple_ref.shape[0]
    key_rows = triple_ref[:, HD : 2 * HD]
    ones = jnp.ones((total, HD), triple_ref.dtype)
    value_rows = jnp.concatenate([triple_ref[:, 2 * HD :], ones], axis=1)
    scale = HD ** (-0.5) * LOG2E
    half = shard_rows // 2
    device = lax.axis_index("seq")
    count = queries_ref.shape[0] // shard_rows

    def shard_of(i):
        return device ^ (i if near else NEAR + i)

    for i in range(count):
        shard = shard_of(i)
        odd = lax.rem(shard, 2)
        for j, at in enumerate((odd, 1 - odd)):
            rows = pl.multiple_of(shard * shard_rows + at * half, 16)
            start = i * shard_rows + j * half
            queries_ref[start : start + half, :] = triple_ref[pl.ds(rows, half), :HD]

    sizes = [size * shard_rows for size in (NEAR_BLOCKS if near else FAR_BLOCKS)]
    bounds = [(sum(sizes[:i]), sum(sizes[: i + 1])) for i in range(len(sizes))]

    def scores_of(start, stop):
        return lax.dot_general(
            queries_ref[start:stop, :],
            key_rows,
            (((1,), (1,)), ((), ())),
            preferred_element_type=jnp.float32,
        )

    def weights_of(scores):
        row_max = jnp.max(scores, axis=-1, keepdims=True)
        return jnp.exp2((scores - row_max) * scale).astype(jnp.bfloat16)

    copies = []

    def send(source, shard):
        copies.append(pltpu.make_async_copy(source, out_ref.at[shard], sems.at[len(copies)]))
        copies[-1].start()

    if not near:
        zeros_ref[...] = jnp.zeros_like(zeros_ref)
        for i in range(NEAR):
            send(zeros_ref, device ^ i)

    def write(start, stop, weights):
        mixed = jnp.dot(weights, value_rows, preferred_element_type=jnp.float32)
        result = mixed[:, :HD] / mixed[:, HD:]
        result_ref[start:stop, :] = result.astype(result_ref.dtype)
        for at in range(start, stop, shard_rows):
            if near:
                out_refs[at // shard_rows][...] = result_ref[at : at + shard_rows, :]
            else:
                send(result_ref.at[at : at + shard_rows, :], shard_of(at // shard_rows))

    scores = scores_of(*bounds[0])
    weights = None
    for i in range(len(bounds)):
        later = scores_of(*bounds[i + 1]) if i + 1 < len(bounds) else None
        newer = weights_of(scores)
        if weights is not None:
            write(*bounds[i - 1], weights)
        scores, weights = later, newer
    write(*bounds[-1], weights)
    for copy in copies:
        copy.wait()


def attend(triples, shard_rows, near):
    total = triples.shape[0]
    shards = total // shard_rows
    whole = pl.BlockSpec(memory_space=pltpu.VMEM)
    if near:
        shape, outs, count, more = (shard_rows, HD), NEAR, NEAR, []
    else:
        more = [pltpu.VMEM((shard_rows, HD), triples.dtype), pltpu.SemaphoreType.DMA((shards,))]
        shape, outs, count = (shards, shard_rows, HD), 1, shards - NEAR
    return pl.pallas_call(
        functools.partial(attend_kernel, near=near, shard_rows=shard_rows),
        out_shape=[jax.ShapeDtypeStruct(shape, triples.dtype)] * outs,
        in_specs=[whole],
        out_specs=[whole if near else pl.BlockSpec(memory_space=pltpu.HBM)] * outs,
        scratch_shapes=[pltpu.VMEM((count * shard_rows, HD), triples.dtype)] * 2 + more,
        compiler_params=pltpu.CompilerParams(vmem_limit_bytes=VMEM_BYTES),
    )(triples)


def assemble_kernel(far_ref, *refs):
    *near_refs, out_ref, sems = refs
    heads = far_ref.shape[0]
    device = lax.axis_index("seq")
    copies = []

    def put(source, head):
        column = pl.multiple_of(head * HD, HD)
        at = len(copies)
        copies.append(pltpu.make_async_copy(source, out_ref.at[:, pl.ds(column, HD)], sems.at[at]))
        copies[-1].start()

    for i in range(NEAR, heads):
        put(far_ref.at[device ^ i], device ^ i)
    for m, ref in enumerate(near_refs):
        put(ref, device ^ m)
    for copy in copies:
        copy.wait()


def assemble(far, near):
    heads, rows, _ = far.shape
    whole = pl.BlockSpec(memory_space=pltpu.VMEM)
    return pl.pallas_call(
        assemble_kernel,
        out_shape=jax.ShapeDtypeStruct((rows, heads * HD), far.dtype),
        in_specs=[whole] * (1 + NEAR),
        out_specs=pl.BlockSpec(memory_space=pltpu.HBM),
        scratch_shapes=[pltpu.SemaphoreType.DMA((heads,))],
        compiler_params=pltpu.CompilerParams(vmem_limit_bytes=VMEM_BYTES),
    )(far, *near)


def local(projected, kept_index):
    device_count = lax.axis_size("seq")
    kept_total = kept_index.shape[0]
    shard_rows = kept_total // device_count
    spill_rows = projected.shape[0] // 4
    across = [(i, i - 1 + 2 * (i % 2)) for i in range(1, device_count - 1)]
    within = [(i, i ^ 1) for i in range(device_count)]
    everything = (0, 1, 2)
    own_parts = [(0, shard_rows, everything), (shard_rows, spill_rows, everything)]
    inter = select_spill(kept_index, projected, spill_rows)
    from_across = lax.ppermute(inter, "seq", across)
    own, intra = select_rows(kept_index, projected, (1, 2, 3), own_parts, 4)
    from_within = lax.ppermute(intra, "seq", within)
    shard_data = own + jnp.concatenate([from_across, from_within], axis=1)
    triples = lax.all_to_all(shard_data, "seq", split_axis=0, concat_axis=0, tiled=True)
    triples = triples.reshape(kept_total, 3 * HD)
    (far,) = attend(triples, shard_rows, False)
    far = lax.all_to_all(far, "seq", split_axis=0, concat_axis=0, tiled=True)
    near = list(attend(triples, shard_rows, True))
    for m in range(1, NEAR):
        near[m] = lax.ppermute(near[m], "seq", [(i, i ^ m) for i in range(device_count)])
    return assemble(far, near)


def solution(mesh):
    return jax.shard_map(
        local,
        mesh=mesh,
        in_specs=(P(("dp", "seq"), None), P("dp")),
        out_specs=P(("dp", "seq"), None),
        check_vma=False,
    )
```

```python
import functools

import jax
import jax.numpy as jnp
from jax import lax
from jax.experimental import pallas as pl
from jax.experimental.pallas import tpu as pltpu
from jax.sharding import PartitionSpec as P

H = 16
HD = 128
CORES = 2
NEAR = 4
NEAR_BLOCKS = (2, 2)
FAR_BLOCKS = (3, 3, 3, 3)
LOG2E = 1.4426950408889634
VMEM_BYTES = 50 * 1024 * 1024


def pick(device, index_ref, start, tokens, count):
    kept = index_ref.shape[0]
    shift = lax.rem(2 * kept - start, kept)
    index = pltpu.roll(jnp.broadcast_to(index_ref[...].reshape(1, kept), (8, kept)), shift, 1)
    index = (index[:, :128] - device * tokens).astype(jnp.float32)
    column = jnp.transpose(index)[:count, :1]
    token = lax.broadcasted_iota(jnp.int32, (count, tokens), 1).astype(jnp.float32)
    return jnp.where(token == column, 1.0, 0.0).astype(jnp.bfloat16)


def spill_kernel(index_ref, tile_ref, out_ref, columns, sems):
    heads, spill, _ = out_ref.shape
    tokens = tile_ref.shape[0]
    kinds, _, width = columns.shape
    copies = []
    for c in range(kinds):
        at = pl.ds(c * width, width)
        copies.append(pltpu.make_async_copy(tile_ref.at[:, at], columns.at[c], sems.at[c]))
        copies[-1].start()
    device = lax.axis_index("seq")
    odd = lax.rem(device, CORES)
    start = (2 * device + odd * 2 + (1 - odd) * -1) * spill
    choice = pick(device, index_ref, start, tokens, spill)
    for c in range(kinds):
        copies[c].wait()
        picked = jnp.dot(choice, columns[c], preferred_element_type=jnp.float32)
        picked = picked.astype(jnp.bfloat16)
        for h in range(heads):
            out_ref[h, :, c * HD : (c + 1) * HD] = picked[:, h * HD : (h + 1) * HD]


def select_spill(kept_index, projected, spill_rows):
    tokens = projected.shape[0]
    vmem = pl.BlockSpec(memory_space=pltpu.VMEM)
    return pl.pallas_call(
        spill_kernel,
        out_shape=jax.ShapeDtypeStruct((H, spill_rows, 3 * HD), projected.dtype),
        in_specs=[vmem, pl.BlockSpec(memory_space=pltpu.HBM)],
        out_specs=vmem,
        scratch_shapes=[
            pltpu.VMEM((3, tokens, H * HD), projected.dtype),
            pltpu.SemaphoreType.DMA((3,)),
        ],
        compiler_params=pltpu.CompilerParams(vmem_limit_bytes=VMEM_BYTES),
    )(kept_index, projected)


def select_kernel(index_ref, q_ref, k_ref, v_ref, *refs, groups, parts):
    *out_refs, choice = refs
    tokens = q_ref.shape[0]
    spill = tokens // 4

    @pl.when(pl.program_id(0) == 0)
    def _():
        device = lax.axis_index("seq")
        odd = lax.rem(device, CORES)
        for i, group in enumerate(groups):
            ahead = odd * (2 - group) + (1 - odd) * (group - 1)
            start = (2 * device + ahead) * spill
            choice[i * spill : (i + 1) * spill, :] = pick(device, index_ref, start, tokens, spill)

    for c, ref in enumerate((q_ref, k_ref, v_ref)):
        picked = jnp.dot(choice[...], ref[...], preferred_element_type=jnp.float32)
        picked = picked.astype(jnp.bfloat16)
        for out_ref, (start, rows, columns) in zip(out_refs, parts):
            if c not in columns:
                continue
            at = columns.index(c) * HD
            for h in range(out_ref.shape[0]):
                out_ref[h, :, at : at + HD] = picked[start : start + rows, h * HD : (h + 1) * HD]


def select_rows(kept_index, projected, groups, parts, steps):
    tokens = projected.shape[0]
    heads = H // steps

    def columns(c):
        return pl.BlockSpec((tokens, heads * HD), lambda g: (0, c * steps + g))

    def by_head(rows, width):
        return pl.BlockSpec((heads, rows, width), lambda g: (g, 0, 0))

    return pl.pallas_call(
        functools.partial(select_kernel, groups=groups, parts=parts),
        out_shape=[
            jax.ShapeDtypeStruct((H, rows, len(cols) * HD), projected.dtype) for _, rows, cols in parts
        ],
        grid=(steps,),
        in_specs=[pl.BlockSpec(kept_index.shape, lambda g: (0,))] + [columns(c) for c in range(3)],
        out_specs=[by_head(rows, len(cols) * HD) for _, rows, cols in parts],
        scratch_shapes=[pltpu.VMEM((len(groups) * tokens // 4, tokens), jnp.bfloat16)],
        compiler_params=pltpu.CompilerParams(vmem_limit_bytes=VMEM_BYTES),
    )(kept_index, projected, projected, projected)


def attend_kernel(triple_ref, *refs, near, shard_rows):
    if near:
        *out_refs, queries_ref, result_ref = refs
    else:
        out_ref, queries_ref, result_ref, zeros_ref, sems = refs
    total = triple_ref.shape[0]
    key_rows = triple_ref[:, HD : 2 * HD]
    ones = jnp.ones((total, HD), triple_ref.dtype)
    value_rows = jnp.concatenate([triple_ref[:, 2 * HD :], ones], axis=1)
    scale = HD ** (-0.5) * LOG2E
    half = shard_rows // 2
    device = lax.axis_index("seq")
    count = queries_ref.shape[0] // shard_rows

    def shard_of(i):
        return device ^ (i if near else NEAR + i)

    for i in range(count):
        shard = shard_of(i)
        odd = lax.rem(shard, 2)
        for j, at in enumerate((odd, 1 - odd)):
            rows = pl.multiple_of(shard * shard_rows + at * half, 16)
            start = i * shard_rows + j * half
            queries_ref[start : start + half, :] = triple_ref[pl.ds(rows, half), :HD]

    sizes = [size * shard_rows for size in (NEAR_BLOCKS if near else FAR_BLOCKS)]
    bounds = [(sum(sizes[:i]), sum(sizes[: i + 1])) for i in range(len(sizes))]

    def scores_of(start, stop):
        return lax.dot_general(
            queries_ref[start:stop, :],
            key_rows,
            (((1,), (1,)), ((), ())),
            preferred_element_type=jnp.float32,
        )

    def weights_of(scores):
        row_max = jnp.max(scores, axis=-1, keepdims=True)
        return jnp.exp2((scores - row_max) * scale).astype(jnp.bfloat16)

    copies = []

    def send(source, shard):
        copies.append(pltpu.make_async_copy(source, out_ref.at[shard], sems.at[len(copies)]))
        copies[-1].start()

    if not near:
        zeros_ref[...] = jnp.zeros_like(zeros_ref)
        for i in range(NEAR):
            send(zeros_ref, device ^ i)

    def write(start, stop, weights):
        mixed = jnp.dot(weights, value_rows, preferred_element_type=jnp.float32)
        result = mixed[:, :HD] / mixed[:, HD:]
        result_ref[start:stop, :] = result.astype(result_ref.dtype)
        for at in range(start, stop, shard_rows):
            if near:
                out_refs[at // shard_rows][...] = result_ref[at : at + shard_rows, :]
            else:
                send(result_ref.at[at : at + shard_rows, :], shard_of(at // shard_rows))

    scores = scores_of(*bounds[0])
    weights = None
    for i in range(len(bounds)):
        later = scores_of(*bounds[i + 1]) if i + 1 < len(bounds) else None
        newer = weights_of(scores)
        if weights is not None:
            write(*bounds[i - 1], weights)
        scores, weights = later, newer
    write(*bounds[-1], weights)
    for copy in copies:
        copy.wait()


def attend(triples, shard_rows, near):
    total = triples.shape[0]
    shards = total // shard_rows
    whole = pl.BlockSpec(memory_space=pltpu.VMEM)
    if near:
        shape, outs, count, more = (shard_rows, HD), NEAR, NEAR, []
    else:
        more = [pltpu.VMEM((shard_rows, HD), triples.dtype), pltpu.SemaphoreType.DMA((shards,))]
        shape, outs, count = (shards, shard_rows, HD), 1, shards - NEAR
    return pl.pallas_call(
        functools.partial(attend_kernel, near=near, shard_rows=shard_rows),
        out_shape=[jax.ShapeDtypeStruct(shape, triples.dtype)] * outs,
        in_specs=[whole],
        out_specs=[whole if near else pl.BlockSpec(memory_space=pltpu.HBM)] * outs,
        scratch_shapes=[pltpu.VMEM((count * shard_rows, HD), triples.dtype)] * 2 + more,
        compiler_params=pltpu.CompilerParams(vmem_limit_bytes=VMEM_BYTES),
    )(triples)


def assemble_kernel(far_ref, *refs):
    *near_refs, out_ref, sems = refs
    heads = far_ref.shape[0]
    device = lax.axis_index("seq")
    copies = []

    def put(source, head):
        column = pl.multiple_of(head * HD, HD)
        at = len(copies)
        copies.append(pltpu.make_async_copy(source, out_ref.at[:, pl.ds(column, HD)], sems.at[at]))
        copies[-1].start()

    for i in range(NEAR, heads):
        put(far_ref.at[device ^ i], device ^ i)
    for m, ref in enumerate(near_refs):
        put(ref, device ^ m)
    for copy in copies:
        copy.wait()


def assemble(far, near):
    heads, rows, _ = far.shape
    whole = pl.BlockSpec(memory_space=pltpu.VMEM)
    return pl.pallas_call(
        assemble_kernel,
        out_shape=jax.ShapeDtypeStruct((rows, heads * HD), far.dtype),
        in_specs=[whole] * (1 + NEAR),
        out_specs=pl.BlockSpec(memory_space=pltpu.HBM),
        scratch_shapes=[pltpu.SemaphoreType.DMA((heads,))],
        compiler_params=pltpu.CompilerParams(vmem_limit_bytes=VMEM_BYTES),
    )(far, *near)


def local(projected, kept_index):
    device_count = lax.axis_size("seq")
    kept_total = kept_index.shape[0]
    shard_rows = kept_total // device_count
    spill_rows = projected.shape[0] // 4
    across = [(i, i - 1 + 2 * (i % 2)) for i in range(1, device_count - 1)]
    within = [(i, i ^ 1) for i in range(device_count)]
    everything = (0, 1, 2)
    own_parts = [(0, shard_rows, everything), (shard_rows, spill_rows, everything)]
    inter = select_spill(kept_index, projected, spill_rows)
    from_across = lax.ppermute(inter, "seq", across)
    own, intra = select_rows(kept_index, projected, (1, 2, 3), own_parts, 4)
    from_within = lax.ppermute(intra, "seq", within)
    shard_data = own + jnp.concatenate([from_across, from_within], axis=1)
    triples = lax.all_to_all(shard_data, "seq", split_axis=0, concat_axis=0, tiled=True)
    triples = triples.reshape(kept_total, 3 * HD)
    (far,) = attend(triples, shard_rows, False)
    far = lax.all_to_all(far, "seq", split_axis=0, concat_axis=0, tiled=True)
    near = list(attend(triples, shard_rows, True))
    for m in range(1, NEAR):
        near[m] = lax.ppermute(near[m], "seq", [(i, i ^ m) for i in range(device_count)])
    return assemble(far, near)


def solution(mesh):
    return jax.shard_map(
        local,
        mesh=mesh,
        in_specs=(P(("dp", "seq"), None), P("dp")),
        out_specs=P(("dp", "seq"), None),
        check_vma=False,
    )
```
